32 devices in a mesh: clip: 2 (over x), frame: 16 (over z, y, core).
Axes of the slice: x: 2, y: 2, z: 4, core: 2. Of those that a mesh axis runs over, the one named last changes fastest.
Arguments:
- cotangent: bfloat16 [32, 64, 512], P(('clip', 'frame')), parts along dimension 0, may hold values from -6 to 6
- q_spatial: bfloat16 [32, 64, 512], P(('clip', 'frame')), parts along dimension 0, may hold values from -48 to 48
- k_spatial: bfloat16 [32, 64, 512], P(('clip', 'frame')), parts along dimension 0, may hold values from -48 to 48
- v_spatial: bfloat16 [32, 64, 512], P(('clip', 'frame')), parts along dimension 0, may hold values from -6 to 6
- q_temporal: bfloat16 [32, 64, 512], P('clip', 'frame'), parts along dimension 0, may hold values from -48 to 48
- k_temporal: bfloat16 [32, 64, 512], P('clip', 'frame'), parts along dimension 0, may hold values from -48 to 48
- v_temporal: bfloat16 [32, 64, 512], P('clip', 'frame'), parts along dimension 0, may hold values from -6 to 6
- w_qkv_spatial: bfloat16 [512, 1536], replicated, may hold values from -0.25 to 0.25
- w_out_spatial: bfloat16 [512, 512], replicated, may hold values from -0.25 to 0.25
- w_qkv_temporal: bfloat16 [512, 1536], replicated, may hold values from -0.25 to 0.25
- w_out_temporal: bfloat16 [512, 512], replicated, may hold values from -0.25 to 0.25
Outputs:
- input_grad: bfloat16 [32, 64, 512], P(('clip', 'frame')), parts along dimension 0
- grad_out_spatial: float32 [1024, 512], P('clip'), parts along dimension 0
- grad_out_temporal: float32 [1024, 512], P('clip'), parts along dimension 0
The draws below stay inside these ranges and needn't reach their ends.
There are 2 independent parts, one for each index of `clip`. The reference program is written for one: setup_inputs(seed, part) draws one part's arguments, and reference() takes and returns one part's arrays. A program takes and returns all parts, laid end to end along the dimension named above; an argument that names none is the same for every part. Nothing has to cross between parts.
All inputs are finite; a program needn't handle non-finite values.
Results may differ from the reference program's by a relative error of at most 0.0079.
Values may be sent and summed in bfloat16 or wider, within the bound.
A program may use at most 64 MiB of HBM per device.

```python
import math
import jax
import jax.numpy as jnp
from jax import lax

D = 512
HEADS = 8
FRAMES = 16
PATCHES = 64


def drawn_pair(key, salt):
    first, second = jax.random.split(jax.random.fold_in(key, salt), 2)
    shape = (FRAMES, PATCHES, D)
    queries = jax.random.normal(first, shape, jnp.float32)
    key_rows = jax.random.normal(second, shape, jnp.float32)
    return (queries, key_rows)


def draw_q_spatial(key, part):
    return drawn_pair(key, 101)[0].astype(jnp.bfloat16)


def draw_k_spatial(key, part):
    return drawn_pair(key, 101)[1].astype(jnp.bfloat16)


def draw_q_temporal(key, part):
    return drawn_pair(key, 202)[0].astype(jnp.bfloat16)


def draw_k_temporal(key, part):
    return drawn_pair(key, 202)[1].astype(jnp.bfloat16)


def level_of(rng, dims, cuts, least, high):
    loudness = 1.0
    for dim, blocks in cuts:
        steps = jax.random.uniform(jax.random.fold_in(jax.random.fold_in(rng, 6), dim), (blocks,), jnp.float32, least / len(cuts), high / len(cuts))
        loudness = loudness * jnp.repeat(jnp.exp(steps), dims[dim] // blocks).reshape((-1,) + (1,) * (len(dims) - 1 - dim))
    return loudness


def normal_values(key, extent, spread, reach, shards=(), dtype=jnp.bfloat16):
    level = level_of(key, extent, shards, -0.22, 0.18) if shards else 1.0
    drawn = jax.random.normal(key, extent, jnp.float32) * spread * level
    return jnp.minimum(jnp.maximum(drawn, -reach), reach).astype(dtype)


def setup_inputs(seed: int = 0, part: int = 0) -> dict:
    seeds = jax.random.split(jax.random.key(seed), 12)
    own_keys = jax.random.split(jax.random.fold_in(seeds[11], part), 12)
    return {
        "cotangent": normal_values(own_keys[0], (FRAMES, PATCHES, D), 1.0, 6.0, ((0, 16),)),
        "q_spatial": draw_q_spatial(jax.random.fold_in(jax.random.fold_in(seeds[11], part), 71), part),
        "k_spatial": draw_k_spatial(jax.random.fold_in(jax.random.fold_in(seeds[11], part), 71), part),
        "v_spatial": normal_values(own_keys[3], (FRAMES, PATCHES, D), 1.0, 6.0, ((0, 16),)),
        "q_temporal": draw_q_temporal(jax.random.fold_in(jax.random.fold_in(seeds[11], part), 71), part),
        "k_temporal": draw_k_temporal(jax.random.fold_in(jax.random.fold_in(seeds[11], part), 71), part),
        "v_temporal": normal_values(own_keys[6], (FRAMES, PATCHES, D), 1.0, 6.0, ((1, 16),)),
        "w_qkv_spatial": normal_values(seeds[7], (D, 3 * D), D ** -0.5, 0.25),
        "w_out_spatial": normal_values(seeds[8], (D, D), D ** -0.5, 0.25),
        "w_qkv_temporal": normal_values(seeds[9], (D, 3 * D), D ** -0.5, 0.25),
        "w_out_temporal": normal_values(seeds[10], (D, D), D ** -0.5, 0.25),
    }


def contract_last(left_side, right_side):
    return lax.dot_general(left_side, right_side, (((1,), (1,)), ((), ())), preferred_element_type=jnp.float32)

def heads_view(array):
    return array.reshape(array.shape[:-1] + (HEADS, D // HEADS))

def attention_back(query_rows, key_rows, value_rows, upstream, score_scale, temporal):
    side_q = 'qbhd' if temporal else 'bqhd'
    side_k = 'kbhd' if temporal else 'bkhd'
    query_f = query_rows.astype(jnp.float32)
    key_f = key_rows.astype(jnp.float32)
    value_f = value_rows.astype(jnp.float32)
    upstream_f = upstream.astype(jnp.float32)
    scores = jnp.einsum(side_q + ',' + side_k + '->bhqk', query_f, key_f) * score_scale
    probs = jax.nn.softmax(scores, axis=-1)
    probs_half = probs.astype(jnp.bfloat16)
    mixed = jnp.einsum('bhqk,' + side_k + '->' + side_q, probs_half.astype(jnp.float32), value_f).astype(jnp.bfloat16)
    d_probs = jnp.einsum(side_q + ',' + side_k + '->bhqk', upstream_f, value_f)
    d_scores = (probs * (d_probs - lax.optimization_barrier(jnp.sum(probs * d_probs, axis=-1, keepdims=True))) * score_scale).astype(jnp.bfloat16)
    grad_query = jnp.einsum('bhqk,' + side_k + '->' + side_q, d_scores.astype(jnp.float32), key_f).astype(jnp.bfloat16)
    grad_key = jnp.einsum('bhqk,' + side_q + '->' + side_k, d_scores.astype(jnp.float32), query_f).astype(jnp.bfloat16)
    grad_value = jnp.einsum('bhqk,' + side_q + '->' + side_k, probs_half.astype(jnp.float32), upstream_f).astype(jnp.bfloat16)
    return (mixed, grad_query, grad_key, grad_value)

def project_back(base_rows, cotangent_parts, weights):
    summed = base_rows.astype(jnp.float32)
    for position in range(3):
        summed = summed + contract_last(cotangent_parts[position], weights[:, position * D:(position + 1) * D])
    return summed

def reference(cotangent, q_spatial, k_spatial, v_spatial, q_temporal, k_temporal, v_temporal, w_qkv_spatial, w_out_spatial, w_qkv_temporal, w_out_temporal):
    score_scale = 1.0 / math.sqrt(D // HEADS)
    flat_rows = cotangent.reshape(-1, D)
    d_mixed = contract_last(flat_rows, w_out_spatial).astype(jnp.bfloat16)
    blocks = FRAMES // 8
    stacked = tuple((array.reshape(blocks, 8, PATCHES, D) for array in (q_spatial, k_spatial, v_spatial, d_mixed.reshape(FRAMES, PATCHES, D))))

    def per_block(items):
        return attention_back(heads_view(items[0]), heads_view(items[1]), heads_view(items[2]), heads_view(items[3]), score_scale, False)
    results = lax.map(per_block, stacked)
    mixed_s, grad_q, grad_k, grad_v = [array.reshape(-1, D) for array in results]
    grad_spatial = jnp.dot(mixed_s.T, flat_rows, preferred_element_type=jnp.float32)
    inner_grad = project_back(flat_rows, (grad_q, grad_k, grad_v), w_qkv_spatial).astype(jnp.bfloat16)
    d_mixed_t = contract_last(inner_grad, w_out_temporal).astype(jnp.bfloat16)
    temporal_out = attention_back(heads_view(q_temporal), heads_view(k_temporal), heads_view(v_temporal), heads_view(d_mixed_t.reshape(FRAMES, PATCHES, D)), score_scale, True)
    mixed_t, tq, tk, tv = [array.reshape(-1, D) for array in temporal_out]
    grad_temporal = jnp.dot(mixed_t.T, inner_grad, preferred_element_type=jnp.float32)
    result = project_back(inner_grad, (tq, tk, tv), w_qkv_temporal).astype(jnp.bfloat16).reshape(FRAMES, PATCHES, D)
    grad_norm = math.sqrt(FRAMES * PATCHES)
    return (result, grad_spatial / grad_norm, grad_temporal / grad_norm)
```

```python
import functools
import math

import jax
import jax.numpy as jnp
from jax import lax
from jax.experimental import pallas as pl
from jax.experimental.pallas import tpu as pltpu
from jax.sharding import PartitionSpec as P

D = 512
HEADS = 8
HEAD_DIM = D // HEADS
LANES = 128
BF16 = jnp.bfloat16
F32 = jnp.float32


def dot_nt(a, b):
    return lax.dot_general(a, b, (((1,), (1,)), ((), ())), preferred_element_type=F32)


def dot_tn(a, b):
    return lax.dot_general(a, b, (((0,), (0,)), ((), ())), preferred_element_type=F32)


def dot_nn(a, b):
    return lax.dot_general(a, b, (((1,), (0,)), ((), ())), preferred_element_type=F32)


def reduce_levels(n):
    levels, stride = [], 1
    for _ in range(2):
        if n // stride > 2 and (n // stride) % 2 == 0:
            levels.append((stride, 2))
            stride *= 2
    levels.append((stride, n // stride))
    return levels


def padded_rows(n):
    return n * 16 * pl.cdiv(D, n * 16)


def head_stack(tile, group_masks):
    return jnp.concatenate([tile * mask for mask in group_masks], axis=0)


def head_select(stacked, tokens, lane):
    out = stacked[:tokens]
    for g in range(1, LANES // HEAD_DIM):
        out = jnp.where(lane >= g * HEAD_DIM, stacked[g * tokens : (g + 1) * tokens], out)
    return out


def attention_forward(q, k, v, scale, group_masks, lane, same):
    tokens = q.shape[0]
    probs, mixed = [], []
    for t in range(D // LANES):
        cols = slice(t * LANES, (t + 1) * LANES)
        scores = dot_nt(k[:, cols], head_stack(q[:, cols], group_masks)) * scale
        if same is not None:
            scores = jnp.where(same, scores, -1e30)
        e = jnp.exp(scores - jnp.max(scores, axis=0, keepdims=True))
        p = e / jnp.sum(e, axis=0, keepdims=True)
        probs.append(p)
        mixed.append(head_select(dot_tn(p.astype(BF16), v[:, cols]), tokens, lane).astype(BF16))
    return probs, jnp.concatenate(mixed, axis=1)


def attention_backward(q, k, v, d_mixed, probs, scale, group_masks, lane):
    tokens = q.shape[0]
    dq, dk, dv = [], [], []
    for t in range(D // LANES):
        cols = slice(t * LANES, (t + 1) * LANES)
        p = probs[t]
        up = head_stack(d_mixed[:, cols], group_masks)
        d_probs = dot_nt(v[:, cols], up)
        row = jnp.sum(p * d_probs, axis=0, keepdims=True)
        d_scores = (p * (d_probs - row) * scale).astype(BF16)
        dq.append(head_select(dot_tn(d_scores, k[:, cols]), tokens, lane).astype(BF16))
        dk.append(dot_nn(d_scores, head_stack(q[:, cols], group_masks)).astype(BF16))
        dv.append(dot_nn(p.astype(BF16), up).astype(BF16))
    return jnp.concatenate(dq + dk + dv, axis=1)


class GradSum:
    def __init__(self, n, me, acc, send, out, recv, sems, divisor):
        self.levels = reduce_levels(n)
        self.me, self.acc, self.send, self.out = me, acc, send, out
        self.recv, self.sems, self.divisor = recv, sems, divisor
        self.rows, self.offsets = [padded_rows(n)], [0]
        for stride, size in self.levels:
            part = self.rows[-1] // size
            self.rows.append(part)
            self.offsets.append(self.offsets[-1] + lax.rem(lax.div(me, stride), size) * part)
        self.pending = None

    def span(self, offset, rows):
        return pl.ds(pl.multiple_of(offset, rows), rows)

    def peers(self, level):
        stride, size = self.levels[level]
        mine = lax.rem(lax.div(self.me, stride), size)
        for d in range(1, size):
            other = lax.rem(mine + d, size)
            yield d, other, self.me + (other - mine) * stride

    def start_reduce(self, level):
        rows = self.rows[level + 1]
        copies = []
        for d, other, device in self.peers(level):
            copy = pltpu.make_async_remote_copy(
                src_ref=self.send.at[self.span(self.offsets[level] + other * rows, rows)],
                dst_ref=self.recv[level].at[d - 1],
                send_sem=self.sems[0].at[level, d - 1],
                recv_sem=self.sems[1].at[level, d - 1],
                device_id={"frame": device},
                device_id_type=pl.DeviceIdType.MESH,
            )
            copy.start()
            copies.append(copy)
        self.pending = copies

    def begin(self, partial):
        self.acc[:D, :] = partial
        self.send[:D, :] = partial.astype(BF16)
        if self.rows[0] > D:
            self.acc[D:, :] = jnp.zeros((self.rows[0] - D, D), F32)
            self.send[D:, :] = jnp.zeros((self.rows[0] - D, D), BF16)
        self.start_reduce(0)

    def finish_reduce(self, level):
        for copy in self.pending:
            copy.wait()
        rows = self.rows[level + 1]
        span = self.span(self.offsets[level + 1], rows)
        total = self.acc[span, :]
        for d, _, _ in self.peers(level):
            total = total + self.recv[level][d - 1].astype(F32)
        if level + 1 < len(self.levels):
            self.acc[span, :] = total
            self.send[span, :] = total.astype(BF16)
            self.start_reduce(level + 1)
        else:
            self.out[span, :] = (total / self.divisor).astype(BF16)
            self.start_gather(level)

    def start_gather(self, level):
        span = self.span(self.offsets[level + 1], self.rows[level + 1])
        copies = []
        for d, _, device in self.peers(level):
            copy = pltpu.make_async_remote_copy(
                src_ref=self.out.at[span],
                dst_ref=self.out.at[span],
                send_sem=self.sems[2].at[level, d - 1],
                recv_sem=self.sems[3].at[level, d - 1],
                device_id={"frame": device},
                device_id_type=pl.DeviceIdType.MESH,
            )
            copy.start()
            copies.append(copy)
        self.pending = copies

    def finish_gather(self, level):
        for copy in self.pending:
            copy.wait()
        if level > 0:
            self.start_gather(level - 1)


def exchange(n, me, source, target, send_sem, recv_sem):
    copies = []
    for d in range(1, n):
        other = lax.rem(me + d, n)
        copy = pltpu.make_async_remote_copy(
            src_ref=source.at[other],
            dst_ref=target.at[me],
            send_sem=send_sem.at[d - 1],
            recv_sem=recv_sem.at[d - 1],
            device_id={"frame": other},
            device_id_type=pl.DeviceIdType.MESH,
        )
        copy.start()
        copies.append(copy)
    target[me] = source[me]
    return copies


def kernel(n, n_levels, scale, norm, *refs):
    inputs, refs = refs[:11], refs[11:]
    result_ref, grad_s_ref, grad_t_ref = refs[:3]
    refs = refs[3:]
    held, refs = refs[:11], refs[11:]
    load_sem, out_a, in_a, out_b, in_b, a_send, a_recv, b_send, b_recv = refs[:9]
    refs = refs[9:]
    acc_s, send_s = refs[:2]
    recv_s, refs = refs[2 : 2 + n_levels], refs[2 + n_levels :]
    sems_s, refs = refs[:4], refs[4:]
    acc_t, send_t = refs[:2]
    recv_t, refs = refs[2 : 2 + n_levels], refs[2 + n_levels :]
    sems_t = refs[:4]

    me = lax.axis_index("frame")
    loads = []
    for i in (1, 2, 3, 0, 8, 4, 5, 6, 7, 10, 9):
        copy = pltpu.make_async_copy(inputs[i], held[i], load_sem.at[i])
        copy.start()
        loads.append((i, copy))
    loads = dict(loads)

    barrier = pltpu.get_barrier_semaphore()
    for d in range(1, n):
        pl.semaphore_signal(
            barrier,
            inc=1,
            device_id={"frame": lax.rem(me + d, n)},
            device_id_type=pl.DeviceIdType.MESH,
        )

    cot_h, qs_h, ks_h, vs_h, qt_h, kt_h, vt_h, wqs_h, wos_h, wqt_h, wot_h = held
    pieces = qt_h.shape[1]
    lane_row = lax.broadcasted_iota(jnp.int32, (1, LANES), 1)
    masks = [
        jnp.where((lane_row >= g * HEAD_DIM) & (lane_row < (g + 1) * HEAD_DIM), 1.0, 0.0).astype(BF16)
        for g in range(LANES // HEAD_DIM)
    ]

    def flat(ref):
        return jnp.concatenate([ref[j].astype(F32) for j in range(ref.shape[0])], axis=0).astype(BF16)

    for i in (1, 2, 3, 0):
        loads[i].wait()
    cot, q_s, k_s, v_s = cot_h[...], qs_h[...], ks_h[...], vs_h[...]
    tokens = cot.shape[0]
    lane = lax.broadcasted_iota(jnp.int32, (tokens, LANES), 1)
    probs_s, mixed_s = attention_forward(q_s, k_s, v_s, scale, masks, lane, None)
    partial_s = dot_tn(mixed_s, cot)
    pl.semaphore_wait(barrier, n - 1)
    sum_s = GradSum(n, me, acc_s, send_s, grad_s_ref, recv_s, sems_s, norm)
    sum_s.begin(partial_s)

    loads[8].wait()
    d_mixed_s = dot_nt(cot, wos_h[...]).astype(BF16)
    parts_s = attention_backward(q_s, k_s, v_s, d_mixed_s, probs_s, scale, masks, lane)
    loads[7].wait()
    d_x1 = (cot.astype(F32) + dot_nt(parts_s, wqs_h[...])).astype(BF16).astype(F32)
    for j in range(n):
        out_a[j] = d_x1[j * pieces : (j + 1) * pieces].astype(BF16)
    sent_a = exchange(n, me, out_a, in_a, a_send, a_recv)

    sum_s.finish_reduce(0)
    for i in (4, 5, 6):
        loads[i].wait()
    q_t, k_t, v_t = flat(qt_h), flat(kt_h), flat(vt_h)
    rows_t = q_t.shape[0]
    groups = LANES // HEAD_DIM
    key_row = lax.broadcasted_iota(jnp.int32, (rows_t, groups * rows_t), 0)
    query_col = lax.broadcasted_iota(jnp.int32, (rows_t, groups * rows_t), 1)
    same = lax.rem(key_row, pieces) == lax.rem(query_col, pieces)
    lane_t = lax.broadcasted_iota(jnp.int32, (rows_t, LANES), 1)
    probs_t, mixed_t = attention_forward(q_t, k_t, v_t, scale, masks, lane_t, same)
    loads[10].wait()
    loads[9].wait()
    if n_levels > 1:
        sum_s.finish_reduce(1)
    for copy in sent_a:
        copy.wait()
    rows = flat(in_a)

    sum_t = GradSum(n, me, acc_t, send_t, grad_t_ref, recv_t, sems_t, norm)
    sum_t.begin(dot_tn(mixed_t, rows))
    d_mixed_t = dot_nt(rows, wot_h[...]).astype(BF16)
    parts_t = attention_backward(q_t, k_t, v_t, d_mixed_t, probs_t, scale, masks, lane_t)
    d_x0 = rows.astype(F32) + dot_nt(parts_t, wqt_h[...])
    for j in range(n):
        out_b[j] = d_x0[j * pieces : (j + 1) * pieces].astype(BF16)
    sent_b = exchange(n, me, out_b, in_b, b_send, b_recv)

    for level in range(n_levels):
        sum_t.finish_reduce(level)
        if level >= 2:
            sum_s.finish_reduce(level)
    for level in reversed(range(n_levels)):
        sum_s.finish_gather(level)
        sum_t.finish_gather(level)
    for copy in sent_b:
        copy.wait()
    result_ref[...] = flat(in_b)


def on_device(n, *args):
    cotangent, q_temporal = args[0], args[4]
    _, pieces, width = q_temporal.shape
    frames_here, patches, _ = cotangent.shape
    tokens = frames_here * patches
    flat_args = [a.reshape(tokens, width) for a in args[:4]] + list(args[4:])
    levels = reduce_levels(n)
    scratch = [pltpu.VMEM(a.shape, a.dtype) for a in flat_args]
    scratch.append(pltpu.SemaphoreType.DMA((len(flat_args),)))
    scratch += [pltpu.VMEM((n, pieces, width), BF16)] * 4
    scratch += [pltpu.SemaphoreType.DMA((n - 1,))] * 4
    widest = max(size for _, size in levels)
    for _ in range(2):
        scratch += [pltpu.VMEM((padded_rows(n), D), F32), pltpu.VMEM((padded_rows(n), D), BF16)]
        rows = padded_rows(n)
        for _, size in levels:
            rows //= size
            scratch.append(pltpu.VMEM((max(size - 1, 1), rows, D), BF16))
        scratch += [pltpu.SemaphoreType.DMA((len(levels), widest))] * 4
    result, grad_s, grad_t = pl.pallas_call(
        functools.partial(
            kernel,
            n,
            len(levels),
            1.0 / math.sqrt(HEAD_DIM),
            math.sqrt(n * tokens),
        ),
        out_shape=(
            jax.ShapeDtypeStruct((tokens, width), BF16),
            jax.ShapeDtypeStruct((padded_rows(n), D), BF16),
            jax.ShapeDtypeStruct((padded_rows(n), D), BF16),
        ),
        in_specs=[pl.BlockSpec(memory_space=pltpu.HBM)] * len(flat_args),
        out_specs=(pl.BlockSpec(memory_space=pltpu.VMEM),) * 3,
        scratch_shapes=scratch,
        compiler_params=pltpu.CompilerParams(
            collective_id=0, has_side_effects=True, vmem_limit_bytes=40 * 1024 * 1024
        ),
    )(*flat_args)
    return (
        result.reshape(frames_here, patches, width),
        grad_s[:D].astype(F32),
        grad_t[:D].astype(F32),
    )


def solution(mesh):
    n = mesh.shape["frame"]
    return jax.shard_map(
        functools.partial(on_device, n),
        mesh=mesh,
        in_specs=(
            P(("clip", "frame"), None, None),
            P(("clip", "frame"), None, None),
            P(("clip", "frame"), None, None),
            P(("clip", "frame"), None, None),
            P("clip", "frame", None),
            P("clip", "frame", None),
            P("clip", "frame", None),
            P(),
            P(),
            P(),
            P(),
        ),
        out_specs=(P(("clip", "frame"), None, None), P("clip", None), P("clip", None)),
        check_vma=False,
    )
```

```python
import functools
import math

import jax
import jax.numpy as jnp
from jax import lax
from jax.experimental import pallas as pl
from jax.experimental.pallas import tpu as pltpu
from jax.sharding import PartitionSpec as P

D = 512
HEADS = 8
HEAD_DIM = D // HEADS
LANES = 128
VMEM_LIMIT = 60 * 1024 * 1024
BF16 = jnp.bfloat16
F32 = jnp.float32


def dot_nt(a, b):
    return lax.dot_general(a, b, (((1,), (1,)), ((), ())), preferred_element_type=F32)


def dot_tn(a, b):
    return lax.dot_general(a, b, (((0,), (0,)), ((), ())), preferred_element_type=F32)


def dot_nn(a, b):
    return lax.dot_general(a, b, (((1,), (0,)), ((), ())), preferred_element_type=F32)


def reduce_levels(n):
    levels, stride = [], 1
    for _ in range(2):
        if n // stride > 2 and (n // stride) % 2 == 0:
            levels.append((stride, 2))
            stride *= 2
    levels.append((stride, n // stride))
    return levels


def padded_rows(n):
    return n * 16 * pl.cdiv(D, n * 16)


def head_stack(tile, group_masks):
    return jnp.concatenate([tile * mask for mask in group_masks], axis=0)


def head_select(stacked, tokens, lane):
    out = stacked[:tokens]
    for g in range(1, LANES // HEAD_DIM):
        out = jnp.where(lane >= g * HEAD_DIM, stacked[g * tokens : (g + 1) * tokens], out)
    return out


def attention_forward(q, k, v, scale, group_masks, lane, same):
    tokens = q.shape[0]
    probs, mixed = [], []
    for t in range(D // LANES):
        cols = slice(t * LANES, (t + 1) * LANES)
        scores = dot_nt(k[:, cols], head_stack(q[:, cols], group_masks)) * scale
        if same is not None:
            scores = jnp.where(same, scores, -1e30)
        e = jnp.exp(scores - jnp.max(scores, axis=0, keepdims=True))
        p = e / jnp.sum(e, axis=0, keepdims=True)
        probs.append(p)
        mixed.append(head_select(dot_tn(p.astype(BF16), v[:, cols]), tokens, lane).astype(BF16))
    return probs, jnp.concatenate(mixed, axis=1)


def attention_backward(q, k, v, d_mixed, probs, scale, group_masks, lane):
    tokens = q.shape[0]
    dq, dk, dv = [], [], []
    for t in range(D // LANES):
        cols = slice(t * LANES, (t + 1) * LANES)
        p = probs[t]
        up = head_stack(d_mixed[:, cols], group_masks)
        d_probs = dot_nt(v[:, cols], up)
        row = jnp.sum(p * d_probs, axis=0, keepdims=True)
        d_scores = (p * (d_probs - row) * scale).astype(BF16)
        dq.append(head_select(dot_tn(d_scores, k[:, cols]), tokens, lane).astype(BF16))
        dk.append(dot_nn(d_scores, head_stack(q[:, cols], group_masks)).astype(BF16))
        dv.append(dot_nn(p.astype(BF16), up).astype(BF16))
    return jnp.concatenate(dq + dk + dv, axis=1)


class GradSum:
    def __init__(self, n, me, acc, send, out, recv, sems, divisor):
        self.levels = reduce_levels(n)
        self.me, self.acc, self.send, self.out = me, acc, send, out
        self.recv, self.sems, self.divisor = recv, sems, divisor
        self.rows, self.offsets = [padded_rows(n)], [0]
        for stride, size in self.levels:
            part = self.rows[-1] // size
            self.rows.append(part)
            self.offsets.append(self.offsets[-1] + lax.rem(lax.div(me, stride), size) * part)
        self.pending = None

    def span(self, offset, rows):
        return pl.ds(pl.multiple_of(offset, rows), rows)

    def peers(self, level):
        stride, size = self.levels[level]
        mine = lax.rem(lax.div(self.me, stride), size)
        for d in range(1, size):
            other = lax.rem(mine + d, size)
            yield d, other, self.me + (other - mine) * stride

    def start_reduce(self, level):
        rows = self.rows[level + 1]
        copies = []
        for d, other, device in self.peers(level):
            copy = pltpu.make_async_remote_copy(
                src_ref=self.send.at[self.span(self.offsets[level] + other * rows, rows)],
                dst_ref=self.recv[level].at[d - 1],
                send_sem=self.sems[0].at[level, d - 1],
                recv_sem=self.sems[1].at[level, d - 1],
                device_id={"frame": device},
                device_id_type=pl.DeviceIdType.MESH,
            )
            copy.start()
            copies.append(copy)
        self.pending = copies

    def begin(self, partial):
        self.acc[:D, :] = partial
        self.send[:D, :] = partial.astype(BF16)
        if self.rows[0] > D:
            self.acc[D:, :] = jnp.zeros((self.rows[0] - D, D), F32)
            self.send[D:, :] = jnp.zeros((self.rows[0] - D, D), BF16)
        self.start_reduce(0)

    def finish_reduce(self, level):
        for copy in self.pending:
            copy.wait()
        rows = self.rows[level + 1]
        span = self.span(self.offsets[level + 1], rows)
        total = self.acc[span, :]
        for d, _, _ in self.peers(level):
            total = total + self.recv[level][d - 1].astype(F32)
        if level + 1 < len(self.levels):
            self.acc[span, :] = total
            self.send[span, :] = total.astype(BF16)
            self.start_reduce(level + 1)
        else:
            self.out[span, :] = (total / self.divisor).astype(BF16)
            self.start_gather(level)

    def start_gather(self, level):
        span = self.span(self.offsets[level + 1], self.rows[level + 1])
        copies = []
        for d, _, device in self.peers(level):
            copy = pltpu.make_async_remote_copy(
                src_ref=self.out.at[span],
                dst_ref=self.out.at[span],
                send_sem=self.sems[2].at[level, d - 1],
                recv_sem=self.sems[3].at[level, d - 1],
                device_id={"frame": device},
                device_id_type=pl.DeviceIdType.MESH,
            )
            copy.start()
            copies.append(copy)
        self.pending = copies

    def finish_gather(self, level):
        for copy in self.pending:
            copy.wait()
        if level > 0:
            self.start_gather(level - 1)


def exchange(n, me, source, target, send_sem, recv_sem):
    copies = []
    for d in range(1, n):
        other = lax.rem(me + d, n)
        copy = pltpu.make_async_remote_copy(
            src_ref=source.at[other],
            dst_ref=target.at[me],
            send_sem=send_sem.at[d - 1],
            recv_sem=recv_sem.at[d - 1],
            device_id={"frame": other},
            device_id_type=pl.DeviceIdType.MESH,
        )
        copy.start()
        copies.append(copy)
    target[me] = source[me]
    return copies


def kernel(n, n_levels, scale, norm, *refs):
    inputs, outputs, refs = refs[:11], refs[11:14], refs[14:]
    held, refs = refs[:11], refs[11:]
    load_sem, store_sem, result, grad_s, grad_t = refs[:5]
    refs = refs[5:]
    out_m, in_m, out_a, in_a, out_b, in_b, m_send, m_recv, a_send, a_recv, b_send, b_recv = refs[:12]
    refs = refs[12:]
    acc_s, send_s = refs[:2]
    recv_s, refs = refs[2 : 2 + n_levels], refs[2 + n_levels :]
    sems_s, refs = refs[:4], refs[4:]
    acc_t, send_t = refs[:2]
    recv_t, refs = refs[2 : 2 + n_levels], refs[2 + n_levels :]
    sems_t = refs[:4]

    me = lax.axis_index("frame")
    barrier = pltpu.get_barrier_semaphore()
    for d in range(1, n):
        pl.semaphore_signal(
            barrier,
            inc=1,
            device_id={"frame": lax.rem(me + d, n)},
            device_id_type=pl.DeviceIdType.MESH,
        )
    loads = {}
    for i in (4, 5, 6, 1, 2, 3, 0, 8, 7, 10, 9):
        loads[i] = pltpu.make_async_copy(inputs[i], held[i], load_sem.at[i])
        loads[i].start()

    cot_h, qs_h, ks_h, vs_h, qt_h, kt_h, vt_h, wqs_h, wos_h, wqt_h, wot_h = held
    pieces = qt_h.shape[1]
    lane_row = lax.broadcasted_iota(jnp.int32, (1, LANES), 1)
    masks = [
        jnp.where((lane_row >= g * HEAD_DIM) & (lane_row < (g + 1) * HEAD_DIM), 1.0, 0.0).astype(BF16)
        for g in range(LANES // HEAD_DIM)
    ]

    def flat(ref):
        return jnp.concatenate([ref[j].astype(F32) for j in range(ref.shape[0])], axis=0).astype(BF16)

    def split(ref, value):
        for j in range(n):
            ref[j] = value[j * pieces : (j + 1) * pieces].astype(BF16)

    for i in (4, 5, 6):
        loads[i].wait()
    q_t, k_t, v_t = flat(qt_h), flat(kt_h), flat(vt_h)
    rows_t = q_t.shape[0]
    groups = LANES // HEAD_DIM
    key_row = lax.broadcasted_iota(jnp.int32, (rows_t, groups * rows_t), 0)
    query_col = lax.broadcasted_iota(jnp.int32, (rows_t, groups * rows_t), 1)
    same = lax.rem(key_row, pieces) == lax.rem(query_col, pieces)
    lane_t = lax.broadcasted_iota(jnp.int32, (rows_t, LANES), 1)
    probs_t, mixed_t = attention_forward(q_t, k_t, v_t, scale, masks, lane_t, same)
    split(out_m, mixed_t.astype(F32))

    for i in (1, 2, 3, 0):
        loads[i].wait()
    cot, q_s, k_s, v_s = cot_h[...], qs_h[...], ks_h[...], vs_h[...]
    tokens = cot.shape[0]
    lane = lax.broadcasted_iota(jnp.int32, (tokens, LANES), 1)
    probs_s, mixed_s = attention_forward(q_s, k_s, v_s, scale, masks, lane, None)
    partial_s = dot_tn(mixed_s, cot)
    pl.semaphore_wait(barrier, n - 1)
    sum_s = GradSum(n, me, acc_s, send_s, grad_s, recv_s, sems_s, norm)
    sum_s.begin(partial_s)
    sent_m = exchange(n, me, out_m, in_m, m_send, m_recv)

    loads[8].wait()
    d_mixed_s = dot_nt(cot, wos_h[...]).astype(BF16)
    parts_s = attention_backward(q_s, k_s, v_s, d_mixed_s, probs_s, scale, masks, lane)
    sum_s.finish_reduce(0)
    loads[7].wait()
    d_x1 = (cot.astype(F32) + dot_nt(parts_s, wqs_h[...])).astype(BF16)
    split(out_a, d_x1.astype(F32))
    sent_a = exchange(n, me, out_a, in_a, a_send, a_recv)

    for copy in sent_m:
        copy.wait()
    sum_t = GradSum(n, me, acc_t, send_t, grad_t, recv_t, sems_t, norm)
    sum_t.begin(dot_tn(flat(in_m), d_x1))
    for level in range(1, n_levels):
        sum_s.finish_reduce(level)
    sum_t.finish_reduce(0)

    loads[10].wait()
    loads[9].wait()
    for copy in sent_a:
        copy.wait()
    rows = flat(in_a)
    d_mixed_t = dot_nt(rows, wot_h[...]).astype(BF16)
    parts_t = attention_backward(q_t, k_t, v_t, d_mixed_t, probs_t, scale, masks, lane_t)
    if n_levels > 1:
        sum_t.finish_reduce(1)
    sum_s.finish_gather(n_levels - 1)
    split(out_b, rows.astype(F32) + dot_nt(parts_t, wqt_h[...]))
    sent_b = exchange(n, me, out_b, in_b, b_send, b_recv)

    for level in range(2, n_levels):
        sum_t.finish_reduce(level)
    for level in reversed(range(n_levels - 1)):
        sum_s.finish_gather(level)
    stores = [pltpu.make_async_copy(grad_s, outputs[1], store_sem.at[1])]
    stores[0].start()
    for copy in sent_b:
        copy.wait()
    result[...] = flat(in_b)
    stores.append(pltpu.make_async_copy(result, outputs[0], store_sem.at[0]))
    stores[1].start()
    for level in reversed(range(n_levels)):
        sum_t.finish_gather(level)
    stores.append(pltpu.make_async_copy(grad_t, outputs[2], store_sem.at[2]))
    stores[2].start()
    for store in stores:
        store.wait()


def finish_kernel(result_in, grad_s_in, grad_t_in, result_out, grad_s_out, grad_t_out, half, full, result, sem_in, sem_out):
    pairs = ((grad_s_in, grad_s_out), (grad_t_in, grad_t_out))
    parts = 2
    rows = D // parts
    loads, stores = [], []
    for g, (source, _) in enumerate(pairs):
        for p in range(parts):
            span = pl.ds(p * rows, rows)
            copy = pltpu.make_async_copy(source.at[span], half.at[g, span], sem_in.at[g, p])
            copy.start()
            loads.append(copy)
    last = pltpu.make_async_copy(result_in, result, sem_in.at[2, 0])
    last.start()
    for g, (_, target) in enumerate(pairs):
        for p in range(parts):
            span = pl.ds(p * rows, rows)
            loads[g * parts + p].wait()
            full[g, span] = half[g, span].astype(F32)
            copy = pltpu.make_async_copy(full.at[g, span], target.at[span], sem_out.at[g, p])
            copy.start()
            stores.append(copy)
    last.wait()
    copy = pltpu.make_async_copy(result, result_out, sem_out.at[2, 0])
    copy.start()
    stores.append(copy)
    for copy in stores:
        copy.wait()


def on_device(n, *args):
    cotangent, q_temporal = args[0], args[4]
    _, pieces, width = q_temporal.shape
    frames_here, patches, _ = cotangent.shape
    tokens = frames_here * patches
    flat_args = [a.reshape(tokens, width) for a in args[:4]] + list(args[4:])
    levels = reduce_levels(n)
    scratch = [pltpu.VMEM(a.shape, a.dtype) for a in flat_args]
    scratch += [pltpu.SemaphoreType.DMA((len(flat_args),)), pltpu.SemaphoreType.DMA((3,))]
    scratch += [pltpu.VMEM((tokens, width), BF16)] + [pltpu.VMEM((padded_rows(n), D), BF16)] * 2
    scratch += [pltpu.VMEM((n, pieces, width), BF16)] * 6
    scratch += [pltpu.SemaphoreType.DMA((n - 1,))] * 6
    widest = max(size for _, size in levels)
    for _ in range(2):
        scratch += [pltpu.VMEM((padded_rows(n), D), F32), pltpu.VMEM((padded_rows(n), D), BF16)]
        rows = padded_rows(n)
        for _, size in levels:
            rows //= size
            scratch.append(pltpu.VMEM((max(size - 1, 1), rows, D), BF16))
        scratch += [pltpu.SemaphoreType.DMA((len(levels), widest))] * 4
    result, grad_s, grad_t = pl.pallas_call(
        functools.partial(
            kernel,
            n,
            len(levels),
            1.0 / math.sqrt(HEAD_DIM),
            math.sqrt(n * tokens),
        ),
        out_shape=(
            jax.ShapeDtypeStruct((tokens, width), BF16),
            jax.ShapeDtypeStruct((padded_rows(n), D), BF16),
            jax.ShapeDtypeStruct((padded_rows(n), D), BF16),
        ),
        in_specs=[pl.BlockSpec(memory_space=pl.ANY)] * len(flat_args),
        out_specs=(pl.BlockSpec(memory_space=pl.ANY),) * 3,
        scratch_shapes=scratch,
        compiler_params=pltpu.CompilerParams(
            collective_id=0, has_side_effects=True, vmem_limit_bytes=VMEM_LIMIT
        ),
    )(*flat_args)
    result, grad_s, grad_t = pl.pallas_call(
        finish_kernel,
        out_shape=(
            jax.ShapeDtypeStruct((tokens, width), BF16),
            jax.ShapeDtypeStruct((D, D), F32),
            jax.ShapeDtypeStruct((D, D), F32),
        ),
        in_specs=[pl.BlockSpec(memory_space=pl.ANY)] * 3,
        out_specs=(pl.BlockSpec(memory_space=pl.ANY),) * 3,
        scratch_shapes=[
            pltpu.VMEM((2, D, D), BF16),
            pltpu.VMEM((2, D, D), F32),
            pltpu.VMEM((tokens, width), BF16),
            pltpu.SemaphoreType.DMA((3, 2)),
            pltpu.SemaphoreType.DMA((3, 2)),
        ],
        compiler_params=pltpu.CompilerParams(vmem_limit_bytes=VMEM_LIMIT),
    )(result, grad_s, grad_t)
    return result.reshape(frames_here, patches, width), grad_s, grad_t


def solution(mesh):
    n = mesh.shape["frame"]
    return jax.shard_map(
        functools.partial(on_device, n),
        mesh=mesh,
        in_specs=(
            P(("clip", "frame"), None, None),
            P(("clip", "frame"), None, None),
            P(("clip", "frame"), None, None),
            P(("clip", "frame"), None, None),
            P("clip", "frame", None),
            P("clip", "frame", None),
            P("clip", "frame", None),
            P(),
            P(),
            P(),
            P(),
        ),
        out_specs=(P(("clip", "frame"), None, None), P("clip", None), P("clip", None)),
        check_vma=False,
    )
```

```python
import functools
import math

import jax
import jax.numpy as jnp
from jax import lax
from jax.experimental import pallas as pl
from jax.experimental.pallas import tpu as pltpu
from jax.sharding import PartitionSpec as P

D = 512
HEADS = 8
HEAD_DIM = D // HEADS
LANES = 128
VMEM_LIMIT = 60 * 1024 * 1024
BF16 = jnp.bfloat16
F32 = jnp.float32


def dot_nt(a, b):
    return lax.dot_general(a, b, (((1,), (1,)), ((), ())), preferred_element_type=F32)


def dot_tn(a, b):
    return lax.dot_general(a, b, (((0,), (0,)), ((), ())), preferred_element_type=F32)


def dot_nn(a, b):
    return lax.dot_general(a, b, (((1,), (0,)), ((), ())), preferred_element_type=F32)


def reduce_levels(n):
    levels, stride = [], 1
    for _ in range(2):
        if n // stride > 2 and (n // stride) % 2 == 0:
            levels.append((stride, 2))
            stride *= 2
    levels.append((stride, n // stride))
    return levels


PARTS = 2
PART = D // PARTS


def padded_rows(n):
    return n * 16 * pl.cdiv(PART, n * 16)


def head_stack(tile, group_masks):
    return jnp.concatenate([tile * mask for mask in group_masks], axis=0)


def head_select(stacked, tokens, lane):
    out = stacked[:tokens]
    for g in range(1, LANES // HEAD_DIM):
        out = jnp.where(lane >= g * HEAD_DIM, stacked[g * tokens : (g + 1) * tokens], out)
    return out


def attention_forward(q, k, v, scale, group_masks, lane, same):
    tokens = q.shape[0]
    probs, mixed = [], []
    for t in range(D // LANES):
        cols = slice(t * LANES, (t + 1) * LANES)
        scores = dot_nt(k[:, cols], head_stack(q[:, cols], group_masks)) * scale
        if same is not None:
            scores = jnp.where(same, scores, -1e30)
        e = jnp.exp(scores - jnp.max(scores, axis=0, keepdims=True))
        p = e / jnp.sum(e, axis=0, keepdims=True)
        probs.append(p)
        mixed.append(head_select(dot_tn(p.astype(BF16), v[:, cols]), tokens, lane).astype(BF16))
    return probs, jnp.concatenate(mixed, axis=1)


def attention_backward(q, k, v, d_mixed, probs, scale, group_masks, lane):
    tokens = q.shape[0]
    dq, dk, dv = [], [], []
    for t in range(D // LANES):
        cols = slice(t * LANES, (t + 1) * LANES)
        p = probs[t]
        up = head_stack(d_mixed[:, cols], group_masks)
        d_probs = dot_nt(v[:, cols], up)
        row = jnp.sum(p * d_probs, axis=0, keepdims=True)
        d_scores = (p * (d_probs - row) * scale).astype(BF16)
        dq.append(head_select(dot_tn(d_scores, k[:, cols]), tokens, lane).astype(BF16))
        dk.append(dot_nn(d_scores, head_stack(q[:, cols], group_masks)).astype(BF16))
        dv.append(dot_nn(p.astype(BF16), up).astype(BF16))
    return jnp.concatenate(dq + dk + dv, axis=1)


class GradSum:
    def __init__(self, n, me, acc, send, out, recv, sems, divisor):
        self.levels = reduce_levels(n)
        self.me, self.acc, self.send, self.out = me, acc, send, out
        self.recv, self.sems, self.divisor = recv, sems, divisor
        self.rows, self.offsets = [padded_rows(n)], [0]
        for stride, size in self.levels:
            part = self.rows[-1] // size
            self.rows.append(part)
            self.offsets.append(self.offsets[-1] + lax.rem(lax.div(me, stride), size) * part)
        self.pending = None

    def span(self, offset, rows):
        return pl.ds(pl.multiple_of(offset, rows), rows)

    def peers(self, level):
        stride, size = self.levels[level]
        mine = lax.rem(lax.div(self.me, stride), size)
        for d in range(1, size):
            other = lax.rem(mine + d, size)
            yield d, other, self.me + (other - mine) * stride

    def start_reduce(self, level):
        rows = self.rows[level + 1]
        copies = []
        for d, other, device in self.peers(level):
            copy = pltpu.make_async_remote_copy(
                src_ref=self.send.at[self.span(self.offsets[level] + other * rows, rows)],
                dst_ref=self.recv[level].at[d - 1],
                send_sem=self.sems[0].at[level, d - 1],
                recv_sem=self.sems[1].at[level, d - 1],
                device_id={"frame": device},
                device_id_type=pl.DeviceIdType.MESH,
            )
            copy.start()
            copies.append(copy)
        self.pending = copies

    def begin(self, partial):
        self.acc[:PART, :] = partial
        self.send[:PART, :] = partial.astype(BF16)
        if self.rows[0] > PART:
            self.acc[PART:, :] = jnp.zeros((self.rows[0] - PART, D), F32)
            self.send[PART:, :] = jnp.zeros((self.rows[0] - PART, D), BF16)
        self.start_reduce(0)

    def finish_reduce(self, level):
        for copy in self.pending:
            copy.wait()
        rows = self.rows[level + 1]
        span = self.span(self.offsets[level + 1], rows)
        total = self.acc[span, :]
        for d, _, _ in self.peers(level):
            total = total + self.recv[level][d - 1].astype(F32)
        if level + 1 < len(self.levels):
            self.acc[span, :] = total
            self.send[span, :] = total.astype(BF16)
            self.start_reduce(level + 1)
        else:
            self.out[span, :] = (total / self.divisor).astype(BF16)
            self.start_gather(level)

    def start_gather(self, level):
        span = self.span(self.offsets[level + 1], self.rows[level + 1])
        copies = []
        for d, _, device in self.peers(level):
            copy = pltpu.make_async_remote_copy(
                src_ref=self.out.at[span],
                dst_ref=self.out.at[span],
                send_sem=self.sems[2].at[level, d - 1],
                recv_sem=self.sems[3].at[level, d - 1],
                device_id={"frame": device},
                device_id_type=pl.DeviceIdType.MESH,
            )
            copy.start()
            copies.append(copy)
        self.pending = copies

    def finish_gather(self, level):
        for copy in self.pending:
            copy.wait()
        if level > 0:
            self.start_gather(level - 1)


def exchange(n, me, source, target, send_sem, recv_sem):
    copies = []
    for d in range(1, n):
        other = lax.rem(me + d, n)
        copy = pltpu.make_async_remote_copy(
            src_ref=source.at[other],
            dst_ref=target.at[me],
            send_sem=send_sem.at[d - 1],
            recv_sem=recv_sem.at[d - 1],
            device_id={"frame": other},
            device_id_type=pl.DeviceIdType.MESH,
        )
        copy.start()
        copies.append(copy)
    target[me] = source[me]
    return copies


def kernel(n, n_levels, scale, norm, *refs):
    inputs, outputs, refs = refs[:11], refs[11:14], refs[14:]
    held, refs = refs[:11], refs[11:]
    load_sem, store_sem, result, grad_s, grad_t = refs[:5]
    refs = refs[5:]
    out_m, in_m, out_a, in_a, out_b, in_b, m_send, m_recv, a_send, a_recv, b_send, b_recv = refs[:12]
    refs = refs[12:]
    me = lax.axis_index("frame")
    streams = []
    for i in range(2 * PARTS):
        acc, send, recv, sems = refs[0], refs[1], refs[2 : 2 + n_levels], refs[2 + n_levels : 6 + n_levels]
        refs = refs[6 + n_levels :]
        out = (grad_s if i < PARTS else grad_t).at[i % PARTS]
        streams.append(GradSum(n, me, acc, send, out, recv, sems, norm))
    sum_s, sum_t = streams[:PARTS], streams[PARTS:]
    last = n_levels - 1

    def begin(sums, mixed, rows):
        for p in range(PARTS):
            sums[p].begin(dot_tn(mixed[:, p * PART : (p + 1) * PART], rows))

    def reduce(sums, level):
        if level < n_levels:
            for part in sums:
                part.finish_reduce(level)

    def gather(sums, level):
        if level >= 0:
            for part in sums:
                part.finish_gather(level)

    barrier = pltpu.get_barrier_semaphore()
    for d in range(1, n):
        pl.semaphore_signal(
            barrier,
            inc=1,
            device_id={"frame": lax.rem(me + d, n)},
            device_id_type=pl.DeviceIdType.MESH,
        )
    loads = {}
    for i in (1, 2, 3, 0, 4, 5, 6, 8, 7, 10, 9):
        loads[i] = pltpu.make_async_copy(inputs[i], held[i], load_sem.at[i])
        loads[i].start()

    cot_h, qs_h, ks_h, vs_h, qt_h, kt_h, vt_h, wqs_h, wos_h, wqt_h, wot_h = held
    pieces = qt_h.shape[1]
    lane_row = lax.broadcasted_iota(jnp.int32, (1, LANES), 1)
    masks = [
        jnp.where((lane_row >= g * HEAD_DIM) & (lane_row < (g + 1) * HEAD_DIM), 1.0, 0.0).astype(BF16)
        for g in range(LANES // HEAD_DIM)
    ]

    def flat(ref):
        return jnp.concatenate([ref[j].astype(F32) for j in range(ref.shape[0])], axis=0).astype(BF16)

    def split(ref, value):
        for j in range(n):
            ref[j] = value[j * pieces : (j + 1) * pieces].astype(BF16)

    for i in (1, 2, 3, 0):
        loads[i].wait()
    cot, q_s, k_s, v_s = cot_h[...], qs_h[...], ks_h[...], vs_h[...]
    tokens = cot.shape[0]
    lane = lax.broadcasted_iota(jnp.int32, (tokens, LANES), 1)
    probs_s, mixed_s = attention_forward(q_s, k_s, v_s, scale, masks, lane, None)
    pl.semaphore_wait(barrier, n - 1)
    begin(sum_s, mixed_s, cot)

    for i in (4, 5, 6):
        loads[i].wait()
    q_t, k_t, v_t = flat(qt_h), flat(kt_h), flat(vt_h)
    rows_t = q_t.shape[0]
    groups = LANES // HEAD_DIM
    key_row = lax.broadcasted_iota(jnp.int32, (rows_t, groups * rows_t), 0)
    query_col = lax.broadcasted_iota(jnp.int32, (rows_t, groups * rows_t), 1)
    same = lax.rem(key_row, pieces) == lax.rem(query_col, pieces)
    lane_t = lax.broadcasted_iota(jnp.int32, (rows_t, LANES), 1)
    probs_t, mixed_t = attention_forward(q_t, k_t, v_t, scale, masks, lane_t, same)
    split(out_m, mixed_t.astype(F32))
    sent_m = exchange(n, me, out_m, in_m, m_send, m_recv)
    reduce(sum_s, 0)

    loads[8].wait()
    d_mixed_s = dot_nt(cot, wos_h[...]).astype(BF16)
    parts_s = attention_backward(q_s, k_s, v_s, d_mixed_s, probs_s, scale, masks, lane)
    reduce(sum_s, 1)
    loads[7].wait()
    d_x1 = (cot.astype(F32) + dot_nt(parts_s, wqs_h[...])).astype(BF16)
    split(out_a, d_x1.astype(F32))
    sent_a = exchange(n, me, out_a, in_a, a_send, a_recv)

    for copy in sent_m:
        copy.wait()
    begin(sum_t, flat(in_m), d_x1)
    reduce(sum_t, 0)
    reduce(sum_s, 2)

    loads[10].wait()
    loads[9].wait()
    for copy in sent_a:
        copy.wait()
    rows = flat(in_a)
    d_mixed_t = dot_nt(rows, wot_h[...]).astype(BF16)
    parts_t = attention_backward(q_t, k_t, v_t, d_mixed_t, probs_t, scale, masks, lane_t)
    reduce(sum_t, 1)
    gather(sum_s, last)
    split(out_b, rows.astype(F32) + dot_nt(parts_t, wqt_h[...]))
    sent_b = exchange(n, me, out_b, in_b, b_send, b_recv)

    reduce(sum_t, 2)
    for level in reversed(range(last)):
        gather(sum_s, level)
    stores = [pltpu.make_async_copy(grad_s, outputs[1], store_sem.at[1])]
    stores[0].start()
    for copy in sent_b:
        copy.wait()
    result[...] = flat(in_b)
    stores.append(pltpu.make_async_copy(result, outputs[0], store_sem.at[0]))
    stores[1].start()
    for level in reversed(range(n_levels)):
        gather(sum_t, level)
    stores.append(pltpu.make_async_copy(grad_t, outputs[2], store_sem.at[2]))
    stores[2].start()
    for store in stores:
        store.wait()


def finish_kernel(result_in, grad_s_in, grad_t_in, result_out, grad_s_out, grad_t_out, half, full, result, sem_in, sem_out):
    pairs = ((grad_s_in, grad_s_out), (grad_t_in, grad_t_out))
    parts, rows = PARTS, PART
    loads, stores = [], []
    for g, (source, _) in enumerate(pairs):
        for p in range(parts):
            span = pl.ds(p * rows, rows)
            copy = pltpu.make_async_copy(source.at[p, pl.ds(0, rows)], half.at[g, span], sem_in.at[g, p])
            copy.start()
            loads.append(copy)
    last = pltpu.make_async_copy(result_in, result, sem_in.at[2, 0])
    last.start()
    for g, (_, target) in enumerate(pairs):
        for p in range(parts):
            span = pl.ds(p * rows, rows)
            loads[g * parts + p].wait()
            full[g, span] = half[g, span].astype(F32)
            copy = pltpu.make_async_copy(full.at[g, span], target.at[span], sem_out.at[g, p])
            copy.start()
            stores.append(copy)
    last.wait()
    copy = pltpu.make_async_copy(result, result_out, sem_out.at[2, 0])
    copy.start()
    stores.append(copy)
    for copy in stores:
        copy.wait()


def on_device(n, *args):
    cotangent, q_temporal = args[0], args[4]
    _, pieces, width = q_temporal.shape
    frames_here, patches, _ = cotangent.shape
    tokens = frames_here * patches
    flat_args = [a.reshape(tokens, width) for a in args[:4]] + list(args[4:])
    levels = reduce_levels(n)
    scratch = [pltpu.VMEM(a.shape, a.dtype) for a in flat_args]
    scratch += [pltpu.SemaphoreType.DMA((len(flat_args),)), pltpu.SemaphoreType.DMA((3,))]
    scratch += [pltpu.VMEM((tokens, width), BF16)] + [pltpu.VMEM((PARTS, padded_rows(n), D), BF16)] * 2
    scratch += [pltpu.VMEM((n, pieces, width), BF16)] * 6
    scratch += [pltpu.SemaphoreType.DMA((n - 1,))] * 6
    widest = max(size for _, size in levels)
    for _ in range(2 * PARTS):
        scratch += [pltpu.VMEM((padded_rows(n), D), F32), pltpu.VMEM((padded_rows(n), D), BF16)]
        rows = padded_rows(n)
        for _, size in levels:
            rows //= size
            scratch.append(pltpu.VMEM((max(size - 1, 1), rows, D), BF16))
        scratch += [pltpu.SemaphoreType.DMA((len(levels), widest))] * 4
    result, grad_s, grad_t = pl.pallas_call(
        functools.partial(
            kernel,
            n,
            len(levels),
            1.0 / math.sqrt(HEAD_DIM),
            math.sqrt(n * tokens),
        ),
        out_shape=(
            jax.ShapeDtypeStruct((tokens, width), BF16),
            jax.ShapeDtypeStruct((PARTS, padded_rows(n), D), BF16),
            jax.ShapeDtypeStruct((PARTS, padded_rows(n), D), BF16),
        ),
        in_specs=[pl.BlockSpec(memory_space=pl.ANY)] * len(flat_args),
        out_specs=(pl.BlockSpec(memory_space=pl.ANY),) * 3,
        scratch_shapes=scratch,
        compiler_params=pltpu.CompilerParams(
            collective_id=0, has_side_effects=True, vmem_limit_bytes=VMEM_LIMIT
        ),
    )(*flat_args)
    result, grad_s, grad_t = pl.pallas_call(
        finish_kernel,
        out_shape=(
            jax.ShapeDtypeStruct((tokens, width), BF16),
            jax.ShapeDtypeStruct((D, D), F32),
            jax.ShapeDtypeStruct((D, D), F32),
        ),
        in_specs=[pl.BlockSpec(memory_space=pl.ANY)] * 3,
        out_specs=(pl.BlockSpec(memory_space=pl.ANY),) * 3,
        scratch_shapes=[
            pltpu.VMEM((2, D, D), BF16),
            pltpu.VMEM((2, D, D), F32),
            pltpu.VMEM((tokens, width), BF16),
            pltpu.SemaphoreType.DMA((3, 2)),
            pltpu.SemaphoreType.DMA((3, 2)),
        ],
        compiler_params=pltpu.CompilerParams(vmem_limit_bytes=VMEM_LIMIT),
    )(result, grad_s, grad_t)
    return result.reshape(frames_here, patches, width), grad_s, grad_t


def solution(mesh):
    n = mesh.shape["frame"]
    return jax.shard_map(
        functools.partial(on_device, n),
        mesh=mesh,
        in_specs=(
            P(("clip", "frame"), None, None),
            P(("clip", "frame"), None, None),
            P(("clip", "frame"), None, None),
            P(("clip", "frame"), None, None),
            P("clip", "frame", None),
            P("clip", "frame", None),
            P("clip", "frame", None),
            P(),
            P(),
            P(),
            P(),
        ),
        out_specs=(P(("clip", "frame"), None, None), P("clip", None), P("clip", None)),
        check_vma=False,
    )
```

```python
import functools
import math

import jax
import jax.numpy as jnp
from jax import lax
from jax.experimental import pallas as pl
from jax.experimental.pallas import tpu as pltpu
from jax.sharding import PartitionSpec as P

D = 512
HEADS = 8
HEAD_DIM = D // HEADS
LANES = 128
VMEM_LIMIT = 60 * 1024 * 1024
BF16 = jnp.bfloat16
F32 = jnp.float32


def dot_nt(a, b):
    return lax.dot_general(a, b, (((1,), (1,)), ((), ())), preferred_element_type=F32)


def dot_tn(a, b):
    return lax.dot_general(a, b, (((0,), (0,)), ((), ())), preferred_element_type=F32)


def dot_nn(a, b):
    return lax.dot_general(a, b, (((1,), (0,)), ((), ())), preferred_element_type=F32)


def reduce_levels(n):
    levels, stride = [], 1
    for _ in range(2):
        if n // stride > 2 and (n // stride) % 2 == 0:
            levels.append((stride, 2))
            stride *= 2
    levels.append((stride, n // stride))
    return levels


PARTS = 2
PART = D // PARTS


def padded_rows(n):
    return n * 16 * pl.cdiv(PART, n * 16)


def head_stack(tile, group_masks):
    return jnp.concatenate([tile * mask for mask in group_masks], axis=0)


def head_select(stacked, tokens, lane):
    out = stacked[:tokens]
    for g in range(1, LANES // HEAD_DIM):
        out = jnp.where(lane >= g * HEAD_DIM, stacked[g * tokens : (g + 1) * tokens], out)
    return out


def attention_forward(q, k, v, scale, group_masks, lane, same):
    tokens = q.shape[0]
    probs, mixed = [], []
    for t in range(D // LANES):
        cols = slice(t * LANES, (t + 1) * LANES)
        scores = dot_nt(k[:, cols], head_stack(q[:, cols], group_masks)) * scale
        if same is not None:
            scores = jnp.where(same, scores, -1e30)
        e = jnp.exp(scores - jnp.max(scores, axis=0, keepdims=True))
        p = e / jnp.sum(e, axis=0, keepdims=True)
        probs.append(p)
        mixed.append(head_select(dot_tn(p.astype(BF16), v[:, cols]), tokens, lane).astype(BF16))
    return probs, jnp.concatenate(mixed, axis=1)


def attention_backward(q, k, v, d_mixed, probs, scale, group_masks, lane):
    tokens = q.shape[0]
    dq, dk, dv = [], [], []
    for t in range(D // LANES):
        cols = slice(t * LANES, (t + 1) * LANES)
        p = probs[t]
        up = head_stack(d_mixed[:, cols], group_masks)
        d_probs = dot_nt(v[:, cols], up)
        row = jnp.sum(p * d_probs, axis=0, keepdims=True)
        d_scores = (p * (d_probs - row) * scale).astype(BF16)
        dq.append(head_select(dot_tn(d_scores, k[:, cols]), tokens, lane).astype(BF16))
        dk.append(dot_nn(d_scores, head_stack(q[:, cols], group_masks)).astype(BF16))
        dv.append(dot_nn(p.astype(BF16), up).astype(BF16))
    return jnp.concatenate(dq + dk + dv, axis=1)


class GradSum:
    def __init__(self, n, me, acc, send, out, recv, sems, divisor):
        self.levels = reduce_levels(n)
        self.me, self.acc, self.send, self.out = me, acc, send, out
        self.recv, self.sems, self.divisor = recv, sems, divisor
        self.rows, self.offsets = [padded_rows(n)], [0]
        for stride, size in self.levels:
            part = self.rows[-1] // size
            self.rows.append(part)
            self.offsets.append(self.offsets[-1] + lax.rem(lax.div(me, stride), size) * part)
        self.pending = None

    def span(self, offset, rows):
        return pl.ds(pl.multiple_of(offset, rows), rows)

    def peers(self, level):
        stride, size = self.levels[level]
        mine = lax.rem(lax.div(self.me, stride), size)
        for d in range(1, size):
            other = lax.rem(mine + d, size)
            yield d, other, self.me + (other - mine) * stride

    def start_reduce(self, level):
        rows = self.rows[level + 1]
        copies = []
        for d, other, device in self.peers(level):
            copy = pltpu.make_async_remote_copy(
                src_ref=self.send.at[self.span(self.offsets[level] + other * rows, rows)],
                dst_ref=self.recv[level].at[d - 1],
                send_sem=self.sems[0].at[level, d - 1],
                recv_sem=self.sems[1].at[level, d - 1],
                device_id={"frame": device},
                device_id_type=pl.DeviceIdType.MESH,
            )
            copy.start()
            copies.append(copy)
        self.pending = copies

    def begin(self, partial):
        self.acc[:PART, :] = partial
        self.send[:PART, :] = partial.astype(BF16)
        if self.rows[0] > PART:
            self.acc[PART:, :] = jnp.zeros((self.rows[0] - PART, D), F32)
            self.send[PART:, :] = jnp.zeros((self.rows[0] - PART, D), BF16)
        self.start_reduce(0)

    def finish_reduce(self, level):
        for copy in self.pending:
            copy.wait()
        rows = self.rows[level + 1]
        span = self.span(self.offsets[level + 1], rows)
        total = self.acc[span, :]
        for d, _, _ in self.peers(level):
            total = total + self.recv[level][d - 1].astype(F32)
        if level + 1 < len(self.levels):
            self.acc[span, :] = total
            self.send[span, :] = total.astype(BF16)
            self.start_reduce(level + 1)
        else:
            self.out[span, :] = (total / self.divisor).astype(BF16)
            self.start_gather(level)

    def start_gather(self, level):
        span = self.span(self.offsets[level + 1], self.rows[level + 1])
        copies = []
        for d, _, device in self.peers(level):
            copy = pltpu.make_async_remote_copy(
                src_ref=self.out.at[span],
                dst_ref=self.out.at[span],
                send_sem=self.sems[2].at[level, d - 1],
                recv_sem=self.sems[3].at[level, d - 1],
                device_id={"frame": device},
                device_id_type=pl.DeviceIdType.MESH,
            )
            copy.start()
            copies.append(copy)
        self.pending = copies

    def finish_gather(self, level):
        for copy in self.pending:
            copy.wait()
        if level > 0:
            self.start_gather(level - 1)


def exchange(n, me, source, target, send_sem, recv_sem):
    copies = []
    for d in range(1, n):
        other = lax.rem(me + d, n)
        copy = pltpu.make_async_remote_copy(
            src_ref=source.at[other],
            dst_ref=target.at[me],
            send_sem=send_sem.at[d - 1],
            recv_sem=recv_sem.at[d - 1],
            device_id={"frame": other},
            device_id_type=pl.DeviceIdType.MESH,
        )
        copy.start()
        copies.append(copy)
    target[me] = source[me]
    return copies


def kernel(n, n_levels, scale, norm, *refs):
    inputs, outputs, refs = refs[:11], refs[11:14], refs[14:]
    held, refs = refs[:11], refs[11:]
    load_sem, store_sem, result, grad_s, grad_t = refs[:5]
    refs = refs[5:]
    out_m, in_m, out_a, in_a, out_b, in_b, m_send, m_recv, a_send, a_recv, b_send, b_recv = refs[:12]
    refs = refs[12:]
    me = lax.axis_index("frame")
    streams = []
    for i in range(2 * PARTS):
        acc, send, recv, sems = refs[0], refs[1], refs[2 : 2 + n_levels], refs[2 + n_levels : 6 + n_levels]
        refs = refs[6 + n_levels :]
        out = (grad_s if i < PARTS else grad_t).at[i % PARTS]
        streams.append(GradSum(n, me, acc, send, out, recv, sems, norm))
    sum_s, sum_t = streams[:PARTS], streams[PARTS:]
    last = n_levels - 1

    def begin(sums, mixed, rows):
        for p in range(PARTS):
            sums[p].begin(dot_tn(mixed[:, p * PART : (p + 1) * PART], rows))

    def reduce(sums, level):
        if level < n_levels:
            for part in sums:
                part.finish_reduce(level)

    def gather(sums, level):
        if level >= 0:
            for part in sums:
                part.finish_gather(level)

    barrier = pltpu.get_barrier_semaphore()
    for d in range(1, n):
        pl.semaphore_signal(
            barrier,
            inc=1,
            device_id={"frame": lax.rem(me + d, n)},
            device_id_type=pl.DeviceIdType.MESH,
        )
    loads = {}
    for i in (1, 2, 3, 0, 4, 5, 6, 8, 7, 10, 9):
        loads[i] = pltpu.make_async_copy(inputs[i], held[i], load_sem.at[i])
        loads[i].start()

    cot_h, qs_h, ks_h, vs_h, qt_h, kt_h, vt_h, wqs_h, wos_h, wqt_h, wot_h = held
    pieces = qt_h.shape[1]
    lane_row = lax.broadcasted_iota(jnp.int32, (1, LANES), 1)
    masks = [
        jnp.where((lane_row >= g * HEAD_DIM) & (lane_row < (g + 1) * HEAD_DIM), 1.0, 0.0).astype(BF16)
        for g in range(LANES // HEAD_DIM)
    ]

    def flat(ref):
        return jnp.concatenate([ref[j].astype(F32) for j in range(ref.shape[0])], axis=0).astype(BF16)

    def split(ref, value):
        for j in range(n):
            ref[j] = value[j * pieces : (j + 1) * pieces].astype(BF16)

    for i in (1, 2, 3, 0):
        loads[i].wait()
    cot, q_s, k_s, v_s = cot_h[...], qs_h[...], ks_h[...], vs_h[...]
    tokens = cot.shape[0]
    lane = lax.broadcasted_iota(jnp.int32, (tokens, LANES), 1)
    probs_s, mixed_s = attention_forward(q_s, k_s, v_s, scale, masks, lane, None)
    pl.semaphore_wait(barrier, n - 1)
    begin(sum_s, mixed_s, cot)

    for i in (4, 5, 6):
        loads[i].wait()
    q_t, k_t, v_t = flat(qt_h), flat(kt_h), flat(vt_h)
    rows_t = q_t.shape[0]
    groups = LANES // HEAD_DIM
    key_row = lax.broadcasted_iota(jnp.int32, (rows_t, groups * rows_t), 0)
    query_col = lax.broadcasted_iota(jnp.int32, (rows_t, groups * rows_t), 1)
    same = lax.rem(key_row, pieces) == lax.rem(query_col, pieces)
    lane_t = lax.broadcasted_iota(jnp.int32, (rows_t, LANES), 1)
    probs_t, mixed_t = attention_forward(q_t, k_t, v_t, scale, masks, lane_t, same)
    split(out_m, mixed_t.astype(F32))
    sent_m = exchange(n, me, out_m, in_m, m_send, m_recv)
    reduce(sum_s, 0)

    loads[8].wait()
    d_mixed_s = dot_nt(cot, wos_h[...]).astype(BF16)
    parts_s = attention_backward(q_s, k_s, v_s, d_mixed_s, probs_s, scale, masks, lane)
    loads[7].wait()
    d_x1 = (cot.astype(F32) + dot_nt(parts_s, wqs_h[...])).astype(BF16)
    split(out_a, d_x1.astype(F32))
    sent_a = exchange(n, me, out_a, in_a, a_send, a_recv)
    reduce(sum_s, 1)

    for copy in sent_m:
        copy.wait()
    begin(sum_t, flat(in_m), d_x1)
    reduce(sum_t, 0)
    reduce(sum_s, 2)

    loads[10].wait()
    loads[9].wait()
    for copy in sent_a:
        copy.wait()
    rows = flat(in_a)
    reduce(sum_t, 1)
    gather(sum_s, last)
    d_mixed_t = dot_nt(rows, wot_h[...]).astype(BF16)
    parts_t = attention_backward(q_t, k_t, v_t, d_mixed_t, probs_t, scale, masks, lane_t)
    split(out_b, rows.astype(F32) + dot_nt(parts_t, wqt_h[...]))
    sent_b = exchange(n, me, out_b, in_b, b_send, b_recv)

    reduce(sum_t, 2)
    gather(sum_s, last - 1)
    gather(sum_t, last)
    for level in reversed(range(last - 1)):
        gather(sum_s, level)
    stores = [pltpu.make_async_copy(grad_s, outputs[1], store_sem.at[1])]
    stores[0].start()
    for copy in sent_b:
        copy.wait()
    result[...] = flat(in_b)
    stores.append(pltpu.make_async_copy(result, outputs[0], store_sem.at[0]))
    stores[1].start()
    for level in reversed(range(last)):
        gather(sum_t, level)
    stores.append(pltpu.make_async_copy(grad_t, outputs[2], store_sem.at[2]))
    stores[2].start()
    for store in stores:
        store.wait()


def finish_kernel(result_in, grad_s_in, grad_t_in, result_out, grad_s_out, grad_t_out, half, full, result, sem_in, sem_out):
    pairs = ((grad_s_in, grad_s_out), (grad_t_in, grad_t_out))
    parts, rows = PARTS, PART
    loads, stores = [], []
    for g, (source, _) in enumerate(pairs):
        for p in range(parts):
            span = pl.ds(p * rows, rows)
            copy = pltpu.make_async_copy(source.at[p, pl.ds(0, rows)], half.at[g, span], sem_in.at[g, p])
            copy.start()
            loads.append(copy)
    last = pltpu.make_async_copy(result_in, result, sem_in.at[2, 0])
    last.start()
    for g, (_, target) in enumerate(pairs):
        for p in range(parts):
            span = pl.ds(p * rows, rows)
            loads[g * parts + p].wait()
            full[g, span] = half[g, span].astype(F32)
            copy = pltpu.make_async_copy(full.at[g, span], target.at[span], sem_out.at[g, p])
            copy.start()
            stores.append(copy)
    last.wait()
    copy = pltpu.make_async_copy(result, result_out, sem_out.at[2, 0])
    copy.start()
    stores.append(copy)
    for copy in stores:
        copy.wait()


def on_device(n, *args):
    cotangent, q_temporal = args[0], args[4]
    _, pieces, width = q_temporal.shape
    frames_here, patches, _ = cotangent.shape
    tokens = frames_here * patches
    flat_args = [a.reshape(tokens, width) for a in args[:4]] + list(args[4:])
    levels = reduce_levels(n)
    scratch = [pltpu.VMEM(a.shape, a.dtype) for a in flat_args]
    scratch += [pltpu.SemaphoreType.DMA((len(flat_args),)), pltpu.SemaphoreType.DMA((3,))]
    scratch += [pltpu.VMEM((tokens, width), BF16)] + [pltpu.VMEM((PARTS, padded_rows(n), D), BF16)] * 2
    scratch += [pltpu.VMEM((n, pieces, width), BF16)] * 6
    scratch += [pltpu.SemaphoreType.DMA((n - 1,))] * 6
    widest = max(size for _, size in levels)
    for _ in range(2 * PARTS):
        scratch += [pltpu.VMEM((padded_rows(n), D), F32), pltpu.VMEM((padded_rows(n), D), BF16)]
        rows = padded_rows(n)
        for _, size in levels:
            rows //= size
            scratch.append(pltpu.VMEM((max(size - 1, 1), rows, D), BF16))
        scratch += [pltpu.SemaphoreType.DMA((len(levels), widest))] * 4
    result, grad_s, grad_t = pl.pallas_call(
        functools.partial(
            kernel,
            n,
            len(levels),
            1.0 / math.sqrt(HEAD_DIM),
            math.sqrt(n * tokens),
        ),
        out_shape=(
            jax.ShapeDtypeStruct((tokens, width), BF16),
            jax.ShapeDtypeStruct((PARTS, padded_rows(n), D), BF16),
            jax.ShapeDtypeStruct((PARTS, padded_rows(n), D), BF16),
        ),
        in_specs=[pl.BlockSpec(memory_space=pl.ANY)] * len(flat_args),
        out_specs=(pl.BlockSpec(memory_space=pl.ANY),) * 3,
        scratch_shapes=scratch,
        compiler_params=pltpu.CompilerParams(
            collective_id=0, has_side_effects=True, vmem_limit_bytes=VMEM_LIMIT
        ),
    )(*flat_args)
    result, grad_s, grad_t = pl.pallas_call(
        finish_kernel,
        out_shape=(
            jax.ShapeDtypeStruct((tokens, width), BF16),
            jax.ShapeDtypeStruct((D, D), F32),
            jax.ShapeDtypeStruct((D, D), F32),
        ),
        in_specs=[pl.BlockSpec(memory_space=pl.ANY)] * 3,
        out_specs=(pl.BlockSpec(memory_space=pl.ANY),) * 3,
        scratch_shapes=[
            pltpu.VMEM((2, D, D), BF16),
            pltpu.VMEM((2, D, D), F32),
            pltpu.VMEM((tokens, width), BF16),
            pltpu.SemaphoreType.DMA((3, 2)),
            pltpu.SemaphoreType.DMA((3, 2)),
        ],
        compiler_params=pltpu.CompilerParams(vmem_limit_bytes=VMEM_LIMIT),
    )(result, grad_s, grad_t)
    return result.reshape(frames_here, patches, width), grad_s, grad_t


def solution(mesh):
    n = mesh.shape["frame"]
    return jax.shard_map(
        functools.partial(on_device, n),
        mesh=mesh,
        in_specs=(
            P(("clip", "frame"), None, None),
            P(("clip", "frame"), None, None),
            P(("clip", "frame"), None, None),
            P(("clip", "frame"), None, None),
            P("clip", "frame", None),
            P("clip", "frame", None),
            P("clip", "frame", None),
            P(),
            P(),
            P(),
            P(),
        ),
        out_specs=(P(("clip", "frame"), None, None), P("clip", None), P("clip", None)),
        check_vma=False,
    )
```
